512 devices in a mesh: row: 16 (over x, z_lo), col: 32 (over z_hi, y, core).
Axes of the slice: x: 4, y: 4, z: 16 (z_hi: 4, z_lo: 4; z = z_hi * 4 + z_lo), core: 2. Of those that a mesh axis runs over, the one named last changes fastest.
Arguments:
- iterate: bfloat16 [5120, 24576], P('row', 'col'), may hold values from -0.0234375 to 0.0234375
Outputs:
- update: float32 [5120, 24576], P('row', 'col')
The draws below stay inside these ranges and needn't reach their ends.
All inputs are finite; a program needn't handle non-finite values.
Results may differ from the reference program's by a relative error of at most 0.0047.
Values may be sent and summed in bfloat16 or wider, within the bound.
A program may use at most 64 MiB of HBM per device.

```python
import jax
import jax.numpy as jnp
from jax import lax

D = 5120
HID = 24576


def levels(rng, dims, cuts, low, largest):
    loudness = 1.0
    for position, shards_of in cuts:
        steps = jax.random.uniform(jax.random.fold_in(jax.random.fold_in(rng, 6), position), (shards_of,), jnp.float32, low / len(cuts), largest / len(cuts))
        loudness = loudness * jnp.repeat(jnp.exp(steps), dims[position] // shards_of).reshape((-1,) + (1,) * (len(dims) - 1 - position))
    return loudness


def centred(own_key, shape, scale, reach, cuts=(), held_as=jnp.bfloat16):
    entries = scale * jax.random.normal(own_key, shape, jnp.float32)
    if cuts:
        entries = entries * levels(own_key, shape, cuts, -0.22, 0.18)
    return jnp.clip(entries, -reach, reach).astype(held_as)


def setup_inputs(seed: int = 0) -> dict:
    key_of = jax.random.split(jax.random.key(seed), 2)
    return {
        "iterate": centred(key_of[0], (D, HID), (HID * 12 // 5) ** -0.5, 0.0234375, ((0, 16), (1, 32))),
    }


def reference(iterate):
    wide = iterate.astype(jnp.float32)
    gram = jnp.dot(wide, wide.T, precision=lax.Precision.HIGHEST, preferred_element_type=jnp.float32).astype(jnp.bfloat16)
    image = jnp.dot(gram.astype(jnp.float32), wide, precision=lax.Precision.HIGHEST, preferred_element_type=jnp.float32).astype(jnp.bfloat16)
    second = jnp.dot(gram.astype(jnp.float32), image.astype(jnp.float32), precision=lax.Precision.HIGHEST, preferred_element_type=jnp.float32)
    factor = 0.2 * (HID ** 0.5)
    return factor * (3.4445 * wide - 4.7750 * image.astype(jnp.float32) + 2.0315 * second)
```

```python
import functools

import jax
import jax.numpy as jnp
from jax import lax
from jax.experimental import pallas as pl
from jax.experimental.pallas import tpu as pltpu
from jax.sharding import PartitionSpec as P

HID = 24576
FACTOR = 0.2 * HID**0.5
MESH = pl.DeviceIdType.MESH
F32 = jnp.float32
BF16 = jnp.bfloat16
NT = (((1,), (1,)), ((), ()))


def pick(index, *values):
    out = values[-1]
    for i in range(len(values) - 2, -1, -1):
        out = jnp.where(index == i, values[i], out)
    return out


def ring(i, distance):
    return lax.rem(i + distance + 4, 4)


def visit(i):
    m = lax.rem(i, 4)
    code = jnp.where(i < 4, jnp.maximum(i - 1, 0), jnp.where(i < 12, m, jnp.where(i < 14, i - 11, 3)))
    middle = lax.div(i, 4) + (m == 0).astype(jnp.int32) - (m == 3).astype(jnp.int32)
    rank = jnp.where(i < 4, (i == 1).astype(jnp.int32), jnp.where(i < 12, middle, jnp.where(i < 14, 3, i - 12)))
    return code, rank


def chain_order(z, t):
    low = jnp.minimum(z, 3 - z)
    base = jnp.where((low == 1) & (t < 2), 1 - t, t)
    return jnp.where(z < 2, base, 3 - base)


def tile_of(zh, y):
    return zh * 4 + ring(y, -zh)


def kernel(
    x_ref, out_ref, xg, own, csend, crecv, ysend, yrecv, zsend, zrecv, gl, gr, ng,
    xs_sem, xr_sem, cs_sem, cr_sem, ys_sem, yr_sem, zs_sem, zr_sem,
    ls_sem, lr_sem, rs_sem, rr_sem, hs_sem, hr_sem, ns_sem, nr_sem, ms_sem, mr_sem,
):
    rows = x_ref.shape[0]
    half = rows // 2
    me = lax.axis_index("row")
    place = lax.axis_index("col")
    x, z = lax.div(me, 4), lax.rem(me, 4)
    zh, y, core = lax.div(place, 8), lax.rem(lax.div(place, 2), 4), lax.rem(place, 2)
    mine = tile_of(zh, y)

    def col_at(a, b):
        return {"col": (a * 4 + b) * 2 + core}

    partner = {"col": (zh * 4 + y) * 2 + 1 - core}

    barrier = pltpu.get_barrier_semaphore()

    def greet(device):
        pl.semaphore_signal(barrier, inc=1, device_id=device, device_id_type=MESH)

    greet({"row": ring(x, 1) * 4 + z})
    greet({"row": ring(x, -1) * 4 + z})
    pl.when(z < 3)(lambda: greet({"row": me + 1}))
    pl.when(z > 0)(lambda: greet({"row": me - 1}))
    greet(partner)
    for d in range(1, 4):
        greet(col_at(zh, ring(y, d)))
        greet(col_at(ring(zh, d), y))
    peers = 9 + (z < 3).astype(jnp.int32) + (z > 0).astype(jnp.int32)
    xg[me] = x_ref[...]
    pl.semaphore_wait(barrier, peers)

    def remote(src, dst, ssem, rsem, device):
        return pltpu.make_async_remote_copy(
            src_ref=src, dst_ref=dst, send_sem=ssem, recv_sem=rsem, device_id=device, device_id_type=MESH
        )

    def row_slot(i):
        code, t = visit(i)
        return pick(code, x, ring(x, -1), ring(x, 1), ring(x, 2)) * 4 + chain_order(z, t)

    def row_ops(full, part, ssem, rsem):
        def send(ref, sem, rcv, target):
            return remote(ref, ref, ssem.at[sem], rcv, {"row": target})

        right, left = ring(x, 1) * 4 + z, ring(x, -1) * 4 + z

        def to_right(slot, b):
            return send(full(slot), 8 + b, rsem.at[slot, 0], right)

        def to_left(slot, b):
            return send(full(slot), 12 + b, rsem.at[slot, 0], left)

        def on_right(slot, b):
            return send(part(slot, 0), 16 + b, rsem.at[slot, 0], right)

        def on_left(slot, b):
            return send(part(slot, 1), 20 + b, rsem.at[slot, 1], left)

        def up(slot, b):
            return send(full(slot), b, rsem.at[slot, 0], me + 1)

        def down(slot, b):
            return send(full(slot), 4 + b, rsem.at[slot, 0], me - 1)

        def step(i):
            code, t = visit(i)
            b = chain_order(z, t)
            slot = row_slot(i)

            @pl.when(((code == 0) & (t > 0)) | (code == 1) | (code == 2))
            def _():
                to_right(slot, b).wait_recv()

            @pl.when(code == 0)
            def _():
                pl.when((b <= z) & (z < 3))(lambda: up(slot, b).start())
                pl.when((b >= z) & (z > 0))(lambda: down(slot, b).start())
                to_right(slot, b).start()
                to_left(slot, b).start()

            pl.when(code == 1)(lambda: on_right(slot, b).start())
            pl.when(code == 2)(lambda: on_left(slot, b).start())

            @pl.when(code == 3)
            def _():
                on_right(slot, b).wait_recv()
                on_left(slot, b).wait_recv()

        def drain():
            def body(b, _):
                slot = x * 4 + b
                pl.when((b <= z) & (z < 3))(lambda: up(slot, b).wait_send())
                pl.when((b >= z) & (z > 0))(lambda: down(slot, b).wait_send())
                to_right(slot, b).wait_send()
                to_left(slot, b).wait_send()
                on_right(slot, b).wait_send()
                on_left(slot, b).wait_send()
                return 0

            lax.fori_loop(0, 4, body, 0)

        return step, drain

    def col_tile(i):
        code, t = visit(i)
        a = pick(t, zh, ring(zh, -1), ring(zh, 1), ring(zh, 2))
        b = pick(code, y, ring(y, -1), ring(y, 1), ring(y, 2))
        return tile_of(a, b)

    def col_ops(full, part, ssem, rsem):
        def send(ref, sem, rcv, target):
            return remote(ref, ref, ssem.at[sem], rcv, target)

        up, down = col_at(ring(zh, 1), y), col_at(ring(zh, -1), y)
        right, left = col_at(zh, ring(y, 1)), col_at(zh, ring(y, -1))

        def z_up(k):
            return send(full(k), 0, rsem.at[k, 0], up)

        def z_down(k):
            return send(full(k), 1, rsem.at[k, 0], down)

        def z_on_up(k):
            return send(part(k, 0), 2, rsem.at[k, 0], up)

        def z_on_down(k):
            return send(part(k, 1), 3, rsem.at[k, 1], down)

        def to_right(k, t):
            return send(full(k), 4 + t, rsem.at[k, 0], right)

        def to_left(k, t):
            return send(full(k), 8 + t, rsem.at[k, 0], left)

        def on_right(k, t):
            return send(part(k, 0), 12 + t, rsem.at[k, 0], right)

        def on_left(k, t):
            return send(part(k, 1), 16 + t, rsem.at[k, 1], left)

        def step(i):
            code, t = visit(i)
            k = col_tile(i)

            @pl.when(((code == 0) & ((t == 1) | (t == 2))) | (code == 1) | (code == 2))
            def _():
                to_right(k, t).wait_recv()

            @pl.when((code == 3) | ((code == 0) & (t == 3)))
            def _():
                on_right(k, t).wait_recv()
                on_left(k, t).wait_recv()

            @pl.when(code == 0)
            def _():
                @pl.when(t == 0)
                def _():
                    z_up(k).start()
                    z_down(k).start()

                pl.when(t == 1)(lambda: z_on_up(k).start())
                pl.when(t == 2)(lambda: z_on_down(k).start())
                to_right(k, t).start()
                to_left(k, t).start()

            pl.when(code == 1)(lambda: on_right(k, t).start())
            pl.when(code == 2)(lambda: on_left(k, t).start())

        def drain():
            for copy in (z_up(mine), z_down(mine), z_on_up(mine), z_on_down(mine)):
                copy.wait_send()

            def body(t, _):
                for copy in (to_right, to_left, on_right, on_left):
                    copy(mine, t).wait_send()
                return 0

            lax.fori_loop(0, 4, body, 0)

        return step, drain

    low = pl.multiple_of(core * half, 32)
    high = pl.multiple_of((1 - core) * half, 32)

    x_step, x_drain = row_ops(
        lambda s: xg.at[s], lambda s, w: xg.at[s, pl.ds(w * half, half)], xs_sem, xr_sem
    )

    def across(k):
        return remote(csend.at[k], crecv.at[k], cs_sem.at[k], cr_sem.at[k], partner)

    def y_send(k, d):
        return remote(
            ysend.at[k], yrecv.at[lax.div(k, 4), d - 1], ys_sem.at[k], yr_sem.at[lax.div(k, 4), d - 1],
            col_at(zh, ring(y, d)),
        )

    def core_sum(k):
        across(k).wait_recv()
        total = own[k] + crecv[k].astype(F32)
        d = ring(lax.div(k, 4) + lax.rem(k, 4), -y)

        @pl.when(lax.rem(d, 4) == 0)
        def _():
            own[k] = total

        @pl.when(lax.rem(d, 4) != 0)
        def _():
            ysend[k] = total.astype(BF16)
            y_send(k, lax.rem(d, 4)).start()

    def z_send(a, d):
        return remote(zsend.at[a], zrecv.at[d - 1], zs_sem.at[a], zr_sem.at[d - 1], col_at(ring(zh, d), y))

    def y_sum(a):
        k = tile_of(a, y)
        total = own[k]
        for d in range(1, 4):
            y_send(a * 4, d).wait_recv()
            total = total + yrecv[a, d - 1].astype(F32)
        d = ring(a, -zh)

        @pl.when(d == 0)
        def _():
            own[k] = total

        @pl.when(d != 0)
        def _():
            zsend[a] = total.astype(BF16)
            z_send(a, d).start()

    def x_body(i, _):
        pl.when(i == 14)(lambda: y_sum(x))

        @pl.when(i == 15)
        def _():
            y_sum(ring(x, -1))
            y_sum(ring(x, 1))

        x_step(i)
        k = row_slot(i)
        csend[k] = lax.dot_general(x_ref[pl.ds(high, half)], xg[k], NT, preferred_element_type=F32).astype(BF16)
        across(k).start()
        own[k] = lax.dot_general(x_ref[pl.ds(low, half)], xg[k], NT, preferred_element_type=F32)
        pl.when(i > 0)(lambda: core_sum(row_slot(i - 1)))
        return 0

    lax.fori_loop(0, 16, x_body, 0)
    core_sum(row_slot(jnp.int32(15)))
    y_sum(ring(x, 2))
    total = own[mine]
    for d in range(1, 4):
        z_send(zh, d).wait_recv()
        total = total + zrecv[d - 1].astype(F32)
    gl[mine] = total.astype(BF16)
    gr[me, pl.ds(low, half)] = total.astype(BF16)

    quarter = half // 2
    l_step, l_drain = col_ops(
        lambda k: gl.at[k], lambda k, w: gl.at[k, pl.ds(w * quarter, quarter)], ls_sem, lr_sem
    )
    r_step, r_drain = row_ops(
        lambda s: gr.at[s, pl.ds(low, half)],
        lambda s, w: gr.at[s, pl.ds(pl.multiple_of(core * half + w * quarter, 16), quarter)],
        rs_sem, rr_sem,
    )

    def halves(ref, s, ssem, rsem):
        return remote(ref.at[s, pl.ds(low, half)], ref.at[s, pl.ds(low, half)], ssem.at[s], rsem.at[s], partner)

    def g_body(i, _):
        l_step(i)
        r_step(i)
        halves(gr, row_slot(i), hs_sem, hr_sem).start()
        return 0

    lax.fori_loop(0, 16, g_body, 0)

    def n_body(k, total):
        halves(gr, k, hs_sem, hr_sem).wait_recv()
        return total + jnp.dot(gl[k], gr[k], preferred_element_type=F32)

    square = lax.fori_loop(0, 16, n_body, jnp.zeros((half, rows), F32))
    ng[mine, pl.ds(low, half)] = (4.775 * gl[mine].astype(F32) - 2.0315 * square).astype(BF16)

    n_step, n_drain = col_ops(
        lambda k: ng.at[k, pl.ds(low, half)],
        lambda k, w: ng.at[k, pl.ds(pl.multiple_of(core * half + w * quarter, 16), quarter)],
        ns_sem, nr_sem,
    )
    out_ref[...] = (FACTOR * 3.4445) * x_ref[...].astype(F32)

    def product(k):
        halves(ng, k, ms_sem, mr_sem).wait_recv()
        out_ref[...] -= FACTOR * jnp.dot(ng[k], xg[k], preferred_element_type=F32)

    def o_body(i, _):
        n_step(i)
        halves(ng, col_tile(i), ms_sem, mr_sem).start()
        pl.when(i > 0)(lambda: product(col_tile(i - 1)))
        return 0

    lax.fori_loop(0, 16, o_body, 0)
    product(col_tile(jnp.int32(15)))

    x_drain()
    l_drain()
    r_drain()
    n_drain()

    def end(k, _):
        across(k).wait_send()
        halves(gr, k, hs_sem, hr_sem).wait_send()
        halves(ng, k, ms_sem, mr_sem).wait_send()
        d = ring(lax.div(k, 4) + lax.rem(k, 4), -y)
        pl.when(lax.rem(d, 4) != 0)(lambda: y_send(k, 1).wait_send())
        return 0

    lax.fori_loop(0, 16, end, 0)

    def z_end(a, _):
        pl.when(a != zh)(lambda: z_send(a, 1).wait_send())
        return 0

    lax.fori_loop(0, 4, z_end, 0)


def local(iterate):
    rows, columns = iterate.shape
    half = rows // 2
    dma = pltpu.SemaphoreType.DMA
    vmem = pltpu.VMEM
    return pl.pallas_call(
        kernel,
        out_shape=jax.ShapeDtypeStruct((rows, columns), F32),
        in_specs=[pl.BlockSpec(memory_space=pltpu.VMEM)],
        out_specs=pl.BlockSpec(memory_space=pltpu.VMEM),
        scratch_shapes=[
            vmem((16, rows, columns), BF16),
            vmem((16, half, rows), F32),
            vmem((16, half, rows), BF16),
            vmem((16, half, rows), BF16),
            vmem((16, half, rows), BF16),
            vmem((4, 3, half, rows), BF16),
            vmem((4, half, rows), BF16),
            vmem((3, half, rows), BF16),
            vmem((16, half, rows), BF16),
            vmem((16, rows, rows), BF16),
            vmem((16, rows, rows), BF16),
            dma((24,)), dma((16, 2)),
            dma((16,)), dma((16,)),
            dma((16,)), dma((4, 3)),
            dma((4,)), dma((3,)),
            dma((20,)), dma((16, 2)),
            dma((24,)), dma((16, 2)),
            dma((16,)), dma((16,)),
            dma((20,)), dma((16, 2)),
            dma((16,)), dma((16,)),
        ],
        compiler_params=pltpu.CompilerParams(
            collective_id=0, has_side_effects=True, vmem_limit_bytes=48 * 2**20
        ),
        name="newton_schulz",
    )(iterate)


def solution(mesh):
    in_specs = (P("row", "col"),)
    out_specs = P("row", "col")
    return jax.shard_map(local, mesh=mesh, in_specs=in_specs, out_specs=out_specs, check_vma=False)
```
